512 devices in a mesh: rep: 8 (over x, core), fsdp: 64 (over y, z).
Axes of the slice: x: 4, y: 8, z: 8, core: 2. Of those that a mesh axis runs over, the one named last changes fastest.
Arguments:
- partials: bfloat16 [8, 8, 30, 512, 512], P('rep', None, None, 'fsdp'), may hold values from -8 to 8
- momentum: float32 [8, 30, 512, 512], P('rep', None, 'fsdp'), may hold values from -6 to 6
- owners: int32 [8, 30], P('rep'), may hold values from 0 to 63, as said below
- factors: bfloat16 [8, 64, 2, 2, 512, 512], P('rep', 'fsdp'), may hold values from -4 to 4
Outputs:
- new_momentum: float32 [8, 30, 512, 512], P('rep', None, 'fsdp')
The draws below stay inside these ranges and needn't reach their ends.
Inputs may be any that keep to these rules, and one draw needn't show every extreme that they name: `owners`: within each group, every index of fsdp owns at most 2 blocks, and one index owns exactly 2.
All inputs are finite; a program needn't handle non-finite values.
Results may differ from the reference program's by a relative error of at most 0.019.
Values may be sent and summed in bfloat16 or wider, within the bound.
A program may use at most 64 MiB of HBM per device.

```python
import math
import jax
import jax.numpy as jnp
from jax import lax

BS = 512
SLOTS = 2
NBG = 30
N_REP = 8
N_FSDP = 64


def draw_partials(key, part):
    key = jax.random.fold_in(key, 11)
    first, second, third = jax.random.split(key, 3)
    shape = (N_REP, N_REP, NBG, BS, BS)
    base = jax.random.normal(first, shape, jnp.float32)
    lowest, highest = (0.3, 3.0)
    row_scale = jnp.exp(jax.random.uniform(second, (1, N_REP, NBG, BS, 1), jnp.float32, math.log(lowest), math.log(highest)))
    col_scale = jnp.exp(jax.random.uniform(third, (1, N_REP, NBG, 1, BS), jnp.float32, math.log(lowest), math.log(highest)))
    return jnp.clip(0.35 * base * row_scale * col_scale, -8.0, 8.0).astype(jnp.bfloat16)


def draw_owners(key, part):
    key = jax.random.fold_in(key, 17)

    def one_group(group_key):
        first, second, third = jax.random.split(group_key, 3)
        heavy = jax.random.randint(first, (), 0, N_FSDP).astype(jnp.int32)
        spread = jax.random.permutation(second, (N_FSDP - 1) * SLOTS)[:NBG - SLOTS].astype(jnp.int32) // SLOTS
        spread = spread + (spread >= heavy).astype(jnp.int32)
        listing = jnp.concatenate([jnp.full((SLOTS,), heavy, jnp.int32), spread])
        return jax.random.permutation(third, listing).astype(jnp.int32)
    return jax.vmap(one_group)(jax.random.split(key, N_REP))


def draw_factors(key, part):
    key = jax.random.fold_in(key, 23)
    first, second = jax.random.split(key, 2)
    shape = (N_REP, N_FSDP, SLOTS, 2, BS, BS)
    diagonal = jnp.exp(jax.random.uniform(first, (N_REP, N_FSDP, SLOTS, 2, BS, 1), jnp.float32, math.log(0.3), math.log(3.0)))
    noise = jnp.clip(jax.random.normal(second, shape, jnp.float32), -6.0, 6.0)
    mixed = (noise + jnp.swapaxes(noise, -1, -2)) * (0.35 / math.sqrt(BS))
    eye = (lax.broadcasted_iota(jnp.int32, (BS, BS), 0) == lax.broadcasted_iota(jnp.int32, (BS, BS), 1)).astype(jnp.float32)
    return (eye * diagonal + (1.0 - eye) * mixed).astype(jnp.bfloat16)


def levels(rng, dims, pieces, low, top_value):
    def one(axis_at, shards_of):
        draws = jax.random.uniform(jax.random.fold_in(jax.random.fold_in(rng, 6), axis_at), (shards_of,), jnp.float32, low / len(pieces), top_value / len(pieces))
        return jnp.repeat(jnp.exp(draws), dims[axis_at] // shards_of).reshape((-1,) + (1,) * (len(dims) - axis_at - 1))

    level = one(*pieces[0])
    for cut in pieces[1:]:
        level = level * one(*cut)
    return level


def centred(own_key, extent, width, bound, cuts=(), dtype=jnp.bfloat16):
    values = width * jax.random.normal(own_key, extent, jnp.float32)
    if cuts:
        values = values * levels(own_key, extent, cuts, -0.22, 0.18)
    return jnp.clip(values, -bound, bound).astype(dtype)


def setup_inputs(seed: int = 0) -> dict:
    keys = jax.random.split(jax.random.key(seed), 5)
    partials = draw_partials(jax.random.fold_in(keys[4], 71), 0)
    momentum = centred(keys[1], (N_REP, NBG, BS, BS), 1.0, 6.0, ((0, 8), (2, 64)), jnp.float32)
    owners = draw_owners(jax.random.fold_in(keys[4], 71), 0)
    factors = draw_factors(jax.random.fold_in(keys[4], 71), 0)
    return {"partials": partials, "momentum": momentum, "owners": owners, "factors": factors}


EPSILON = 1e-06
BETA = 0.9

def reference(partials, momentum, owners, factors):
    results = []
    for group in range(N_REP):
        grad = lax.optimization_barrier(jnp.sum(partials[:, group].astype(jnp.float32), axis=0)).astype(jnp.bfloat16)
        owned = owners[group].astype(jnp.int32)
        same = owned[:, None] == owned[None, :]
        earlier = lax.broadcasted_iota(jnp.int32, (NBG, NBG), 1) < lax.broadcasted_iota(jnp.int32, (NBG, NBG), 0)
        slot = lax.optimization_barrier(jnp.sum((same & earlier).astype(jnp.int32), axis=1)).astype(jnp.int32)
        chosen = factors[group][owned, slot]
        left = jnp.einsum('bij,bjk->bik', chosen[:, 0].astype(jnp.float32), grad.astype(jnp.float32)).astype(jnp.bfloat16)
        precond = jnp.einsum('bij,bjk->bik', left.astype(jnp.float32), chosen[:, 1].astype(jnp.float32))
        wide = grad.astype(jnp.float32)
        grad_sq = lax.optimization_barrier(jnp.sum(wide * wide, axis=(1, 2)))
        prec_sq = lax.optimization_barrier(jnp.sum(precond * precond, axis=(1, 2)))
        ratio = jnp.sqrt(grad_sq / (prec_sq + EPSILON))
        update = (precond * ratio[:, None, None]).astype(jnp.bfloat16)
        results.append(BETA * momentum[group] + update.astype(jnp.float32))
    return jnp.stack(results)
```

```python
import functools

import jax
import jax.numpy as jnp
from jax import lax
from jax.experimental import pallas as pl
from jax.experimental.pallas import tpu as pltpu
from jax.sharding import PartitionSpec as P

EPSILON = 1e-06
BETA = 0.9
MESH = pl.DeviceIdType.MESH
F32 = jnp.float32
BF16 = jnp.bfloat16


def iota(shape, dim):
    return lax.broadcasted_iota(jnp.int32, shape, dim)


def kernel(
    nodes, count, rows, width, slots,
    owners, part, fac, out,
    sib, psum, own, xin, grad, pick_out, pick_in, held, out1, in1, left, prec, out2, in2,
    sib_send, sib_recv, x_send, x_recv, send1, recv1, send2, recv2, fac_sem,
):
    rep = lax.axis_index("rep")
    me = lax.axis_index("fsdp")
    chip, core = rep // 2, lax.rem(rep, 2)
    chips = part.shape[0]
    cols = width // 2
    quarter = width // 4
    lines = count * rows

    barrier = pltpu.get_barrier_semaphore()
    pl.semaphore_signal(
        barrier, inc=1, device_id={"rep": chip * 2 + 1 - core}, device_id_type=MESH
    )
    for k in range(1, chips):
        pl.semaphore_signal(
            barrier, inc=1, device_id={"rep": lax.rem(chip + k, chips) * 2 + core},
            device_id_type=MESH,
        )

    def greet(k, carry):
        pl.semaphore_signal(
            barrier, inc=1, device_id={"fsdp": lax.rem(me + k, nodes)}, device_id_type=MESH
        )
        return carry

    lax.fori_loop(1, nodes, greet, 0)
    pl.semaphore_wait(barrier, 1 + chips - 1 + nodes - 1)

    def to_sibling(h):
        return pltpu.make_async_remote_copy(
            src_ref=part.at[:, 1 - core, :, pl.ds(h * cols, cols)],
            dst_ref=sib.at[h],
            send_sem=sib_send.at[h],
            recv_sem=sib_recv.at[h],
            device_id={"rep": chip * 2 + 1 - core},
            device_id_type=MESH,
        )

    for h in range(2):
        to_sibling(h).start()
    load = pltpu.make_async_copy(fac, held, fac_sem)
    load.start()

    lane_block = iota((32, lines), 1) // rows
    sub = iota((32, lines), 0)
    own_lane = jnp.zeros((32, lines), jnp.int32)
    own_sub = jnp.full((32, lines), -1, jnp.int32)
    for b in range(count):
        own_lane = jnp.where(lane_block == b, owners[0, b], own_lane)
        own_sub = jnp.where(sub == b, owners[0, b], own_sub)
    earlier = (own_lane == own_sub) & (sub < lane_block)
    slot_lane = jnp.sum(earlier.astype(jnp.int32), axis=0, keepdims=True)
    place = own_lane[0:1] * rows + lax.rem(iota((1, lines), 1), rows)
    for s in range(slots):
        here = jnp.where(slot_lane == s, place, -1)
        match = iota((nodes * rows, lines), 0) == here
        pick_out[s] = jnp.where(match, 1.0, 0.0).astype(BF16)
    row_block = iota((lines, 128), 0) // rows
    lane = iota((lines, 128), 1)
    own_row = jnp.zeros((lines, 128), jnp.int32)
    own_other = jnp.full((lines, 128), -1, jnp.int32)
    for b in range(count):
        own_row = jnp.where(row_block == b, owners[0, b], own_row)
        own_other = jnp.where(lane == b, owners[0, b], own_other)
    earlier = (own_row == own_other) & (lane < row_block)
    slot_row = jnp.sum(earlier.astype(jnp.int32), axis=1, keepdims=True)
    place = own_row[:, 0:1] * rows + lax.rem(iota((lines, 1), 0), rows)
    for s in range(slots):
        here = jnp.where(slot_row == s, place, -1)
        match = iota((lines, nodes * rows), 1) == here
        pick_in[s] = jnp.where(match, 1.0, 0.0).astype(BF16)

    def to_chip(h, k):
        other = lax.rem(chip + k, chips)
        return pltpu.make_async_remote_copy(
            src_ref=psum.at[h, k - 1],
            dst_ref=xin.at[h, k - 1],
            send_sem=x_send.at[h],
            recv_sem=x_recv.at[h],
            device_id={"rep": other * 2 + core},
            device_id_type=MESH,
        )

    for h in range(2):
        side = pl.ds(h * cols, cols)
        to_sibling(h).wait_recv()
        for k in (2, 1, 3):
            other = lax.rem(chip + k, chips)
            mine = part[other, core, :, side].astype(F32)
            psum[h, k - 1] = (mine + sib[h, other].astype(F32)).astype(BF16)
            to_chip(h, k).start()
        own[h] = part[chip, core, :, side].astype(F32) + sib[h, chip].astype(F32)

    def send_loop(source, target, send, recv):
        def one(k, carry):
            p = lax.rem(me + k, nodes)
            pltpu.make_async_remote_copy(
                src_ref=source.at[p],
                dst_ref=target.at[me],
                send_sem=send,
                recv_sem=recv,
                device_id={"fsdp": p},
                device_id_type=MESH,
            ).start()
            return carry

        lax.fori_loop(1, nodes, one, 0)

    def bulk(source, target, send, recv):
        most = pl.ds(0, nodes - 1)
        return pltpu.make_async_remote_copy(
            src_ref=source.at[most],
            dst_ref=target.at[most],
            send_sem=send,
            recv_sem=recv,
            device_id={"fsdp": lax.rem(me + 1, nodes)},
            device_id_type=MESH,
        )

    def pack(s, h):
        step = 16

        def some(i, carry):
            which = pl.ds(pl.multiple_of(i * step * rows, step * rows), step * rows)
            picked = jnp.dot(pick_out[s, which, :], grad[h], preferred_element_type=F32)
            one = picked[:, :quarter].reshape(step, rows, quarter)
            two = picked[:, quarter:].reshape(step, rows, quarter)
            out1[s, h, pl.ds(i * step, step)] = jnp.concatenate([one, two], axis=1).astype(BF16)
            return carry

        lax.fori_loop(0, nodes // step, some, 0)
        in1[s, h, me] = out1[s, h, me]

    def send_grad(s, h):
        send_loop(out1.at[s, h], in1.at[s, h], send1.at[s, h], recv1.at[s, h])

    for h in range(2):
        pltpu.make_async_remote_copy(
            src_ref=psum.at[h], dst_ref=xin.at[h], send_sem=x_send.at[h], recv_sem=x_recv.at[h],
            device_id={"rep": chip * 2 + 1 - core}, device_id_type=MESH,
        ).wait_recv()
        total = own[h]
        for k in range(chips - 1):
            total = total + xin[h, k].astype(F32)
        grad[h] = total.astype(BF16)
        pack(0, h)
        send_grad(0, h)
        if h == 0:
            pack(1, 0)
    send_grad(1, 0)
    pack(1, 1)
    send_grad(1, 1)
    load.wait()

    for s in range(slots):
        grad_sq = jnp.zeros((1, 1), F32)
        for h in range(2):
            bulk(out1.at[s, h], in1.at[s, h], send1.at[s, h], recv1.at[s, h]).wait_recv()
            wide = in1[s, h].astype(F32)
            grad_sq = grad_sq + jnp.sum(wide * wide, keepdims=True).reshape(1, 1)
            one = wide[:, :rows].reshape(nodes * rows, quarter)
            two = wide[:, rows:].reshape(nodes * rows, quarter)
            block = jnp.concatenate([one, two], axis=1).astype(BF16)
            left[:, h * cols : (h + 1) * cols] = jnp.dot(
                held[s, 0], block, preferred_element_type=F32
            ).astype(BF16)
        prec[...] = jnp.dot(left[...], held[s, 1], preferred_element_type=F32)
        prec_sq = jnp.sum(prec[...] * prec[...], keepdims=True).reshape(1, 1)
        ratio = jnp.sqrt(grad_sq / (prec_sq + EPSILON))
        update = prec[...] * ratio
        one = update[:, :cols].reshape(nodes, rows, cols)
        two = update[:, cols:].reshape(nodes, rows, cols)
        out2[s] = jnp.concatenate([one, two], axis=1).astype(BF16)
        in2[s, me] = out2[s, me]
        send_loop(out2.at[s], in2.at[s], send2.at[s], recv2.at[s])

    for s in range(slots):
        bulk(out2.at[s], in2.at[s], send2.at[s], recv2.at[s]).wait_recv()
        wide = in2[s].astype(F32)
        for h in range(2):
            rows_h = wide[:, h * rows : (h + 1) * rows].reshape(nodes * rows, cols).astype(BF16)
            got = jnp.dot(pick_in[s], rows_h, preferred_element_type=F32)
            if s == 0:
                own[h] = got
            else:
                out[:, h * cols : (h + 1) * cols] = (own[h] + got).astype(BF16)

    for h in range(2):
        to_sibling(h).wait_send()
        pltpu.make_async_remote_copy(
            src_ref=psum.at[h], dst_ref=xin.at[h], send_sem=x_send.at[h], recv_sem=x_recv.at[h],
            device_id={"rep": chip * 2 + 1 - core}, device_id_type=MESH,
        ).wait_send()
    for s in range(slots):
        for h in range(2):
            bulk(out1.at[s, h], in1.at[s, h], send1.at[s, h], recv1.at[s, h]).wait_send()
        bulk(out2.at[s], in2.at[s], send2.at[s], recv2.at[s]).wait_send()


def local(partials, momentum, owners, factors):
    nodes = lax.axis_size("fsdp")
    slots = factors.shape[2]
    groups, count, rows, width = partials.shape[1:]
    lines = count * rows
    chips = groups // 2
    cols = width // 2
    vmem, dma = pltpu.VMEM, pltpu.SemaphoreType.DMA
    update = pl.pallas_call(
        functools.partial(kernel, nodes, count, rows, width, slots),
        out_shape=jax.ShapeDtypeStruct((lines, width), BF16),
        in_specs=[
            pl.BlockSpec(memory_space=pltpu.SMEM),
            pl.BlockSpec(memory_space=pltpu.VMEM),
            pl.BlockSpec(memory_space=pl.ANY),
        ],
        out_specs=pl.BlockSpec(memory_space=pltpu.VMEM),
        scratch_shapes=[
            vmem((2, chips, lines, cols), BF16),
            vmem((2, chips - 1, lines, cols), BF16),
            vmem((2, lines, cols), F32),
            vmem((2, chips - 1, lines, cols), BF16),
            vmem((2, lines, cols), BF16),
            vmem((slots, nodes * rows, lines), BF16),
            vmem((slots, lines, nodes * rows), BF16),
            vmem((slots, 2, width, width), BF16),
            vmem((slots, 2, nodes, 2 * rows, width // 4), BF16),
            vmem((slots, 2, nodes, 2 * rows, width // 4), BF16),
            vmem((width, width), BF16),
            vmem((width, width), F32),
            vmem((slots, nodes, 2 * rows, cols), BF16),
            vmem((slots, nodes, 2 * rows, cols), BF16),
            dma((2,)), dma((2,)), dma((2,)), dma((2,)),
            dma((slots, 2)), dma((slots, 2)), dma((slots,)), dma((slots,)),
            dma,
        ],
        compiler_params=pltpu.CompilerParams(
            collective_id=0, has_side_effects=True, vmem_limit_bytes=48 << 20
        ),
    )(owners, partials.reshape(chips, 2, lines, width), factors[0, 0])
    return BETA * momentum + update.astype(F32).reshape(momentum.shape)


def solution(mesh):
    placed = (
        P("rep", None, None, "fsdp", None),
        P("rep", None, "fsdp", None),
        P("rep", None),
        P("rep", "fsdp", None, None, None, None),
    )
    return jax.shard_map(
        local, mesh=mesh, in_specs=placed, out_specs=P("rep", None, "fsdp", None), check_vma=False
    )
```

```python
import functools

import jax
import jax.numpy as jnp
from jax import lax
from jax.experimental import pallas as pl
from jax.experimental.pallas import tpu as pltpu
from jax.sharding import PartitionSpec as P

EPSILON = 1e-06
BETA = 0.9
MESH = pl.DeviceIdType.MESH
F32 = jnp.float32
BF16 = jnp.bfloat16


def iota(shape, dim):
    return lax.broadcasted_iota(jnp.int32, shape, dim)


def kernel(
    nodes, count, rows, width, slots,
    own_hbm, part, fac, out,
    owners, mine, sib0, sib1, sib2, psum0, psum1, psum2, own0, own1, own2, xin0, xin1, xin2,
    grad0, grad1, grad2, pick_both, pick_one, pick_in, held, outa, ina, outb, inb,
    block, left, prec, out2, in2, picked,
    sib_send, sib_recv, x_send, x_recv, senda, recva, sendb, recvb, send2, recv2,
    part_sem, fac_sem, own_sem,
):
    rep = lax.axis_index("rep")
    me = lax.axis_index("fsdp")
    chip, core = rep // 2, lax.rem(rep, 2)
    chips = part.shape[0]
    quarter = width // 4
    cols = width // 2
    lines = count * rows
    whole = nodes * rows
    sibling = {"rep": chip * 2 + 1 - core}
    spans = ((0, quarter), (quarter, quarter), (cols, cols))
    sib, psum, own = (sib0, sib1, sib2), (psum0, psum1, psum2), (own0, own1, own2)
    xin, grad = (xin0, xin1, xin2), (grad0, grad1, grad2)

    def fetch(i):
        side = pl.ds(*spans[i])
        return pltpu.make_async_copy(
            part.at[:, core, :, side], mine.at[:, :, side], part_sem.at[i]
        )

    for i in range(3):
        fetch(i).start()
    ids = pltpu.make_async_copy(own_hbm, owners, own_sem)
    ids.start()

    barrier = pltpu.get_barrier_semaphore()
    pl.semaphore_signal(barrier, inc=1, device_id=sibling, device_id_type=MESH)
    for k in range(1, chips):
        pl.semaphore_signal(
            barrier, inc=1, device_id={"rep": lax.rem(chip + k, chips) * 2 + core},
            device_id_type=MESH,
        )

    def greet(k, carry):
        pl.semaphore_signal(
            barrier, inc=1, device_id={"fsdp": lax.rem(me + k, nodes)}, device_id_type=MESH
        )
        return carry

    lax.fori_loop(1, nodes, greet, 0)
    pl.semaphore_wait(barrier, 1 + chips - 1 + nodes - 1)

    def to_sibling(i):
        return pltpu.make_async_remote_copy(
            src_ref=part.at[:, 1 - core, :, pl.ds(*spans[i])],
            dst_ref=sib[i],
            send_sem=sib_send.at[i],
            recv_sem=sib_recv.at[i],
            device_id=sibling,
            device_id_type=MESH,
        )

    for i in range(3):
        to_sibling(i).start()
    load = pltpu.make_async_copy(fac, held, fac_sem)
    load.start()

    def to_chip(i, k):
        return pltpu.make_async_remote_copy(
            src_ref=psum[i].at[k - 1],
            dst_ref=xin[i].at[k - 1],
            send_sem=x_send.at[i],
            recv_sem=x_recv.at[i],
            device_id={"rep": lax.rem(chip + k, chips) * 2 + core},
            device_id_type=MESH,
        )

    def x_bulk(i):
        return pltpu.make_async_remote_copy(
            src_ref=psum[i], dst_ref=xin[i], send_sem=x_send.at[i], recv_sem=x_recv.at[i],
            device_id=sibling, device_id_type=MESH,
        )

    def pair_sums(i):
        side = pl.ds(*spans[i])
        to_sibling(i).wait_recv()
        fetch(i).wait()
        for k in (2, 1, 3):
            other = lax.rem(chip + k, chips)
            pair = mine[other, :, side].astype(F32) + sib[i][other].astype(F32)
            psum[i][k - 1] = pair.astype(BF16)
            to_chip(i, k).start()
        own[i][...] = mine[chip, :, side].astype(F32) + sib[i][chip].astype(F32)

    def total(i):
        x_bulk(i).wait_recv()
        if i + 1 < 3:
            pair_sums(i + 1)
        acc = own[i][...]
        for k in range(chips - 1):
            acc = acc + xin[i][k].astype(F32)
        grad[i][...] = acc.astype(BF16)

    def send_loop(source, target, send, recv):
        def one(k, carry):
            p = lax.rem(me + k, nodes)
            pltpu.make_async_remote_copy(
                src_ref=source.at[p],
                dst_ref=target.at[me],
                send_sem=send,
                recv_sem=recv,
                device_id={"fsdp": p},
                device_id_type=MESH,
            ).start()
            return carry

        lax.fori_loop(1, nodes, one, 0)

    def bulk(source, target, send, recv):
        most = pl.ds(0, nodes - 1)
        return pltpu.make_async_remote_copy(
            src_ref=source.at[most],
            dst_ref=target.at[most],
            send_sem=send,
            recv_sem=recv,
            device_id={"fsdp": lax.rem(me + 1, nodes)},
            device_id_type=MESH,
        )

    ids.wait()
    lane_block = iota((32, lines), 1) // rows
    sub = iota((32, lines), 0)

    def spread(b, carry):
        lanes, subs = carry
        o = owners[0, b]
        return jnp.where(lane_block == b, o, lanes), jnp.where(sub == b, o, subs)

    own_lane, own_sub = lax.fori_loop(
        0, count, spread, (jnp.zeros((32, lines), jnp.int32), jnp.full((32, lines), -1, jnp.int32))
    )
    earlier = (own_lane == own_sub) & (sub < lane_block)
    slot_lane = jnp.sum(earlier.astype(jnp.int32), axis=0, keepdims=True)
    row_lane = lax.rem(iota((1, lines), 1), rows)
    place = (own_lane[0:1] * slots + slot_lane) * rows + row_lane
    step = 2 * rows * 4

    pair_sums(0)

    def build(i, carry):
        first = pl.multiple_of(i * step, step)
        match = iota((step, lines), 0) + first == place
        pick_both[pl.ds(first, step), :] = jnp.where(match, 1.0, 0.0).astype(BF16)
        return carry

    lax.fori_loop(0, slots * whole // step, build, 0)
    place_one = own_lane[0:1] * rows + row_lane
    for s in range(slots):
        here = jnp.where(slot_lane == s, place_one, -1)

        def build_one(i, carry, s=s, here=here):
            first = pl.multiple_of(i * step, step)
            match = iota((step, lines), 0) + first == here
            pick_one[s, pl.ds(first, step), :] = jnp.where(match, 1.0, 0.0).astype(BF16)
            return carry

        lax.fori_loop(0, whole // step, build_one, 0)

    for i in range(2):
        total(i)
        outa[i] = jnp.dot(pick_both[...], grad[i][...], preferred_element_type=F32).reshape(
            nodes, slots * rows, quarter
        ).astype(BF16)
        ina[i, me] = outa[i, me]
        send_loop(outa.at[i], ina.at[i], senda.at[i], recva.at[i])
    total(2)
    for s in range(slots):
        picked[...] = jnp.dot(pick_one[s], grad[2][...], preferred_element_type=F32)
        one = picked[:, :quarter].reshape(nodes, rows, quarter)
        two = picked[:, quarter:].reshape(nodes, rows, quarter)
        outb[s] = jnp.concatenate([one, two], axis=1).astype(BF16)
        inb[s, me] = outb[s, me]
        send_loop(outb.at[s], inb.at[s], sendb.at[s], recvb.at[s])

    row_block = iota((lines, 128), 0) // rows
    lane = iota((lines, 128), 1)

    def spread_rows(b, carry):
        mine_rows, others = carry
        o = owners[0, b]
        return jnp.where(row_block == b, o, mine_rows), jnp.where(lane == b, o, others)

    own_row, own_other = lax.fori_loop(
        0, count, spread_rows,
        (jnp.zeros((lines, 128), jnp.int32), jnp.full((lines, 128), -1, jnp.int32)),
    )
    earlier = (own_row == own_other) & (lane < row_block)
    slot_row = jnp.sum(earlier.astype(jnp.int32), axis=1, keepdims=True)
    place_row = own_row[:, 0:1] * rows + lax.rem(iota((lines, 1), 0), rows)
    for s in range(slots):
        here = jnp.where(slot_row == s, place_row, -1)
        match = iota((lines, whole), 1) == here
        pick_in[s] = jnp.where(match, 1.0, 0.0).astype(BF16)
    load.wait()

    squares = [jnp.zeros((rows, quarter), F32) for _ in range(slots)]
    for i in range(2):
        bulk(outa.at[i], ina.at[i], senda.at[i], recva.at[i]).wait_recv()
        for s in range(slots):
            wide = ina[i][:, s * rows : (s + 1) * rows].astype(F32)
            squares[s] = squares[s] + jnp.sum(wide * wide, axis=0)
            block[s, :, i * quarter : (i + 1) * quarter] = wide.reshape(whole, quarter).astype(BF16)
    for s in range(slots):
        left[s, :, :cols] = jnp.dot(
            held[s, 0], block[s, :, :cols], preferred_element_type=F32
        ).astype(BF16)
    for s in range(slots):
        bulk(outb.at[s], inb.at[s], sendb.at[s], recvb.at[s]).wait_recv()
        for q in range(2):
            wide = inb[s][:, q * rows : (q + 1) * rows].astype(F32)
            squares[s] = squares[s] + jnp.sum(wide * wide, axis=0)
            block[s, :, cols + q * quarter : cols + (q + 1) * quarter] = wide.reshape(
                whole, quarter
            ).astype(BF16)
        left[s, :, cols:] = jnp.dot(
            held[s, 0], block[s, :, cols:], preferred_element_type=F32
        ).astype(BF16)
        prec[...] = jnp.dot(left[s], held[s, 1], preferred_element_type=F32)
        prec_sq = jnp.sum(prec[...] * prec[...], keepdims=True).reshape(1, 1)
        grad_sq = jnp.sum(squares[s], keepdims=True).reshape(1, 1)
        ratio = jnp.sqrt(grad_sq / (prec_sq + EPSILON))
        update = prec[...] * ratio
        one = update[:, :cols].reshape(nodes, rows, cols)
        two = update[:, cols:].reshape(nodes, rows, cols)
        out2[s] = jnp.concatenate([one, two], axis=1).astype(BF16)
        in2[s, me] = out2[s, me]
        send_loop(out2.at[s], in2.at[s], send2.at[s], recv2.at[s])

    for s in range(slots):
        bulk(out2.at[s], in2.at[s], send2.at[s], recv2.at[s]).wait_recv()
        for h in range(2):
            rows_h = in2[s][:, h * rows : (h + 1) * rows].astype(F32).reshape(whole, cols)
            got = jnp.dot(pick_in[s], rows_h.astype(BF16), preferred_element_type=F32)
            if s == 0:
                prec[h * lines : (h + 1) * lines, :cols] = got
            else:
                got = got + prec[h * lines : (h + 1) * lines, :cols]
                out[:, h * cols : (h + 1) * cols] = got.astype(BF16)

    for i in range(3):
        to_sibling(i).wait_send()
        x_bulk(i).wait_send()
    for s in range(2):
        bulk(outa.at[s], ina.at[s], senda.at[s], recva.at[s]).wait_send()
        bulk(outb.at[s], inb.at[s], sendb.at[s], recvb.at[s]).wait_send()
        bulk(out2.at[s], in2.at[s], send2.at[s], recv2.at[s]).wait_send()


def local(partials, momentum, owners, factors):
    nodes = lax.axis_size("fsdp")
    slots = factors.shape[2]
    groups, count, rows, width = partials.shape[1:]
    lines = count * rows
    chips = groups // 2
    cols, quarter = width // 2, width // 4
    whole = nodes * rows
    widths = (quarter, quarter, cols)
    vmem, dma = pltpu.VMEM, pltpu.SemaphoreType.DMA
    update = pl.pallas_call(
        functools.partial(kernel, nodes, count, rows, width, slots),
        out_shape=jax.ShapeDtypeStruct((lines, width), BF16),
        in_specs=[
            pl.BlockSpec(memory_space=pltpu.HBM),
            pl.BlockSpec(memory_space=pltpu.HBM),
            pl.BlockSpec(memory_space=pltpu.HBM),
        ],
        out_specs=pl.BlockSpec(memory_space=pltpu.VMEM),
        scratch_shapes=[
            pltpu.SMEM((1, count), jnp.int32),
            vmem((chips, lines, width), BF16),
            *[vmem((chips, lines, w), BF16) for w in widths],
            *[vmem((chips - 1, lines, w), BF16) for w in widths],
            *[vmem((lines, w), F32) for w in widths],
            *[vmem((chips - 1, lines, w), BF16) for w in widths],
            *[vmem((lines, w), BF16) for w in widths],
            vmem((slots * whole, lines), BF16),
            vmem((slots, whole, lines), BF16),
            vmem((slots, lines, whole), BF16),
            vmem((slots, 2, width, width), BF16),
            vmem((2, nodes, slots * rows, quarter), BF16),
            vmem((2, nodes, slots * rows, quarter), BF16),
            vmem((slots, nodes, 2 * rows, quarter), BF16),
            vmem((slots, nodes, 2 * rows, quarter), BF16),
            vmem((slots, width, width), BF16),
            vmem((slots, width, width), BF16),
            vmem((width, width), F32),
            vmem((slots, nodes, 2 * rows, cols), BF16),
            vmem((slots, nodes, 2 * rows, cols), BF16),
            vmem((whole, cols), F32),
            dma((3,)), dma((3,)), dma((3,)), dma((3,)),
            dma((2,)), dma((2,)), dma((slots,)), dma((slots,)), dma((slots,)), dma((slots,)),
            dma((3,)), dma, dma,
        ],
        compiler_params=pltpu.CompilerParams(
            collective_id=0, has_side_effects=True, vmem_limit_bytes=60 << 20
        ),
    )(owners, partials.reshape(chips, 2, lines, width), factors[0, 0])
    return BETA * momentum + update.astype(F32).reshape(momentum.shape)


def solution(mesh):
    placed = (
        P("rep", None, None, "fsdp", None),
        P("rep", None, "fsdp", None),
        P("rep", None),
        P("rep", "fsdp", None, None, None, None),
    )
    return jax.shard_map(
        local, mesh=mesh, in_specs=placed, out_specs=P("rep", None, "fsdp", None), check_vma=False
    )
```

```python
import functools

import jax
import jax.numpy as jnp
from jax import lax
from jax.experimental import pallas as pl
from jax.experimental.pallas import tpu as pltpu
from jax.sharding import PartitionSpec as P

EPSILON = 1e-06
BETA = 0.9
MESH = pl.DeviceIdType.MESH
F32 = jnp.float32
BF16 = jnp.bfloat16


def iota(shape, dim):
    return lax.broadcasted_iota(jnp.int32, shape, dim)


def kernel(
    nodes, count, rows, width, slots,
    own_hbm, part, fac, out,
    owners, mine, sib0, sib1, sib2, psum0, psum1, psum2, own0, own1, own2, xin0, xin1, xin2,
    grad0, grad1, grad2, pick_both, pick_one, pick_in, held, outa, ina, outb, inb,
    block, left, prec, out2, in2, picked,
    sib_send, sib_recv, x_send, x_recv, senda, recva, sendb, recvb, send2, recv2,
    part_sem, fac_sem, own_sem, line_sem,
):
    rep = lax.axis_index("rep")
    me = lax.axis_index("fsdp")
    chip, core = rep // 2, lax.rem(rep, 2)
    chips = part.shape[0]
    side = 8
    quarter = width // 4
    cols = width // 2
    lines = count * rows
    whole = nodes * rows
    sibling = {"rep": chip * 2 + 1 - core}
    spans = ((0, quarter), (quarter, quarter), (cols, cols))
    sib, psum, own = (sib0, sib1, sib2), (psum0, psum1, psum2), (own0, own1, own2)
    xin, grad = (xin0, xin1, xin2), (grad0, grad1, grad2)

    def fetch(i):
        span = pl.ds(*spans[i])
        return pltpu.make_async_copy(
            part.at[:, core, :, span], mine.at[:, :, span], part_sem.at[i]
        )

    for i in range(3):
        fetch(i).start()
    ids = pltpu.make_async_copy(own_hbm, owners, own_sem)
    ids.start()

    barrier = pltpu.get_barrier_semaphore()
    pl.semaphore_signal(barrier, inc=1, device_id=sibling, device_id_type=MESH)
    for k in range(1, chips):
        pl.semaphore_signal(
            barrier, inc=1, device_id={"rep": lax.rem(chip + k, chips) * 2 + core},
            device_id_type=MESH,
        )

    y, z = me // side, lax.rem(me, side)

    def along_y(k):
        return lax.rem(y + k, side) * side + z

    def along_z(k):
        return y * side + lax.rem(z + k, side)

    for k in range(1, side):
        for peer in (along_z(k), along_y(k)):
            pl.semaphore_signal(
                barrier, inc=1, device_id={"fsdp": peer}, device_id_type=MESH
            )
    pl.semaphore_wait(barrier, 1 + chips - 1 + 2 * (side - 1))

    def to_sibling(i):
        return pltpu.make_async_remote_copy(
            src_ref=part.at[:, 1 - core, :, pl.ds(*spans[i])],
            dst_ref=sib[i],
            send_sem=sib_send.at[i],
            recv_sem=sib_recv.at[i],
            device_id=sibling,
            device_id_type=MESH,
        )

    for i in range(3):
        to_sibling(i).start()
    for k in range(1, side):
        pl.semaphore_signal(
            line_sem, inc=1, device_id={"fsdp": along_y(k)}, device_id_type=MESH
        )
    load = pltpu.make_async_copy(fac, held, fac_sem)
    load.start()

    def to_chip(i, k):
        return pltpu.make_async_remote_copy(
            src_ref=psum[i].at[k - 1],
            dst_ref=xin[i].at[k - 1],
            send_sem=x_send.at[i],
            recv_sem=x_recv.at[i],
            device_id={"rep": lax.rem(chip + k, chips) * 2 + core},
            device_id_type=MESH,
        )

    def x_bulk(i):
        return pltpu.make_async_remote_copy(
            src_ref=psum[i], dst_ref=xin[i], send_sem=x_send.at[i], recv_sem=x_recv.at[i],
            device_id=sibling, device_id_type=MESH,
        )

    def pair_sums(i):
        span = pl.ds(*spans[i])
        to_sibling(i).wait_recv()
        fetch(i).wait()
        for k in (2, 1, 3):
            other = lax.rem(chip + k, chips)
            pair = mine[other, :, span].astype(F32) + sib[i][other].astype(F32)
            psum[i][k - 1] = pair.astype(BF16)
            to_chip(i, k).start()
        own[i][...] = mine[chip, :, span].astype(F32) + sib[i][chip].astype(F32)

    def total(i):
        x_bulk(i).wait_recv()
        if i + 1 < 3:
            pair_sums(i + 1)
        acc = own[i][...]
        for k in range(chips - 1):
            acc = acc + xin[i][k].astype(F32)
        grad[i][...] = acc.astype(BF16)

    def send_loop(source, target, send, recv):
        def one(k, carry):
            p = lax.rem(me + k, nodes)
            pltpu.make_async_remote_copy(
                src_ref=source.at[p],
                dst_ref=target.at[me],
                send_sem=send,
                recv_sem=recv,
                device_id={"fsdp": p},
                device_id_type=MESH,
            ).start()
            return carry

        lax.fori_loop(1, nodes, one, 0)

    def bulk(source, target, send, recv):
        most = pl.ds(0, nodes - 1)
        return pltpu.make_async_remote_copy(
            src_ref=source.at[most],
            dst_ref=target.at[most],
            send_sem=send,
            recv_sem=recv,
            device_id={"fsdp": lax.rem(me + 1, nodes)},
            device_id_type=MESH,
        )

    ids.wait()
    lane_block = iota((32, lines), 1) // rows
    sub = iota((32, lines), 0)

    def spread(b, carry):
        lanes, subs = carry
        o = owners[0, b]
        return jnp.where(lane_block == b, o, lanes), jnp.where(sub == b, o, subs)

    own_lane, own_sub = lax.fori_loop(
        0, count, spread, (jnp.zeros((32, lines), jnp.int32), jnp.full((32, lines), -1, jnp.int32))
    )
    earlier = (own_lane == own_sub) & (sub < lane_block)
    slot_lane = jnp.sum(earlier.astype(jnp.int32), axis=0, keepdims=True)
    row_lane = lax.rem(iota((1, lines), 1), rows)
    place = (own_lane[0:1] * slots + slot_lane) * rows + row_lane
    step = 2 * rows * 4

    pair_sums(0)

    def build(i, carry):
        first = pl.multiple_of(i * step, step)
        match = iota((step, lines), 0) + first == place
        pick_both[pl.ds(first, step), :] = jnp.where(match, 1.0, 0.0).astype(BF16)
        return carry

    lax.fori_loop(0, slots * whole // step, build, 0)
    place_one = own_lane[0:1] * rows + row_lane
    for s in range(slots):
        here = jnp.where(slot_lane == s, place_one, -1)

        def build_one(i, carry, s=s, here=here):
            first = pl.multiple_of(i * step, step)
            match = iota((step, lines), 0) + first == here
            pick_one[s, pl.ds(first, step), :] = jnp.where(match, 1.0, 0.0).astype(BF16)
            return carry

        lax.fori_loop(0, whole // step, build_one, 0)

    pl.semaphore_wait(line_sem, side - 1)

    for i in range(2):
        total(i)
        outa[i] = jnp.dot(pick_both[...], grad[i][...], preferred_element_type=F32).reshape(
            nodes, slots * rows, quarter
        ).astype(BF16)
        ina[i, me] = outa[i, me]
        send_loop(outa.at[i], ina.at[i], senda.at[i], recva.at[i])
    total(2)
    for s in range(slots):
        picked[...] = jnp.dot(pick_one[s], grad[2][...], preferred_element_type=F32)
        one = picked[:, :quarter].reshape(nodes, rows, quarter)
        two = picked[:, quarter:].reshape(nodes, rows, quarter)
        outb[s] = jnp.concatenate([one, two], axis=1).astype(BF16)
        inb[s, me] = outb[s, me]
        send_loop(outb.at[s], inb.at[s], sendb.at[s], recvb.at[s])

    row_block = iota((lines, 128), 0) // rows
    lane = iota((lines, 128), 1)

    def spread_rows(b, carry):
        mine_rows, others = carry
        o = owners[0, b]
        return jnp.where(row_block == b, o, mine_rows), jnp.where(lane == b, o, others)

    own_row, own_other = lax.fori_loop(
        0, count, spread_rows,
        (jnp.zeros((lines, 128), jnp.int32), jnp.full((lines, 128), -1, jnp.int32)),
    )
    earlier = (own_row == own_other) & (lane < row_block)
    slot_row = jnp.sum(earlier.astype(jnp.int32), axis=1, keepdims=True)
    place_row = own_row[:, 0:1] * rows + lax.rem(iota((lines, 1), 0), rows)
    for s in range(slots):
        here = jnp.where(slot_row == s, place_row, -1)
        match = iota((lines, whole), 1) == here
        pick_in[s] = jnp.where(match, 1.0, 0.0).astype(BF16)
    load.wait()

    squares = [jnp.zeros((rows, quarter), F32) for _ in range(slots)]
    for i in range(2):
        bulk(outa.at[i], ina.at[i], senda.at[i], recva.at[i]).wait_recv()
        for s in range(slots):
            wide = ina[i][:, s * rows : (s + 1) * rows].astype(F32)
            squares[s] = squares[s] + jnp.sum(wide * wide, axis=0)
            block[s, :, i * quarter : (i + 1) * quarter] = wide.reshape(whole, quarter).astype(BF16)
    for s in range(slots):
        left[s, :, :cols] = jnp.dot(
            held[s, 0], block[s, :, :cols], preferred_element_type=F32
        ).astype(BF16)
    for s in range(slots):
        bulk(outb.at[s], inb.at[s], sendb.at[s], recvb.at[s]).wait_recv()
        for q in range(2):
            wide = inb[s][:, q * rows : (q + 1) * rows].astype(F32)
            squares[s] = squares[s] + jnp.sum(wide * wide, axis=0)
            block[s, :, cols + q * quarter : cols + (q + 1) * quarter] = wide.reshape(
                whole, quarter
            ).astype(BF16)
        left[s, :, cols:] = jnp.dot(
            held[s, 0], block[s, :, cols:], preferred_element_type=F32
        ).astype(BF16)
        prec[...] = jnp.dot(left[s], held[s, 1], preferred_element_type=F32)
        prec_sq = jnp.sum(prec[...] * prec[...], keepdims=True).reshape(1, 1)
        grad_sq = jnp.sum(squares[s], keepdims=True).reshape(1, 1)
        ratio = jnp.sqrt(grad_sq / (prec_sq + EPSILON))
        update = prec[...] * ratio
        one = update[:, :cols].reshape(nodes, rows, cols)
        two = update[:, cols:].reshape(nodes, rows, cols)
        out2[s] = jnp.concatenate([one, two], axis=1).astype(BF16)
        in2[s, me] = out2[s, me]
        send_loop(out2.at[s], in2.at[s], send2.at[s], recv2.at[s])

    for s in range(slots):
        bulk(out2.at[s], in2.at[s], send2.at[s], recv2.at[s]).wait_recv()
        for h in range(2):
            rows_h = in2[s][:, h * rows : (h + 1) * rows].astype(F32).reshape(whole, cols)
            got = jnp.dot(pick_in[s], rows_h.astype(BF16), preferred_element_type=F32)
            if s == 0:
                prec[h * lines : (h + 1) * lines, :cols] = got
            else:
                got = got + prec[h * lines : (h + 1) * lines, :cols]
                out[:, h * cols : (h + 1) * cols] = got.astype(BF16)

    for i in range(3):
        to_sibling(i).wait_send()
        x_bulk(i).wait_send()
    for s in range(2):
        bulk(outa.at[s], ina.at[s], senda.at[s], recva.at[s]).wait_send()
        bulk(outb.at[s], inb.at[s], sendb.at[s], recvb.at[s]).wait_send()
        bulk(out2.at[s], in2.at[s], send2.at[s], recv2.at[s]).wait_send()


def local(partials, momentum, owners, factors):
    nodes = lax.axis_size("fsdp")
    slots = factors.shape[2]
    groups, count, rows, width = partials.shape[1:]
    lines = count * rows
    chips = groups // 2
    cols, quarter = width // 2, width // 4
    whole = nodes * rows
    widths = (quarter, quarter, cols)
    vmem, dma = pltpu.VMEM, pltpu.SemaphoreType.DMA
    update = pl.pallas_call(
        functools.partial(kernel, nodes, count, rows, width, slots),
        out_shape=jax.ShapeDtypeStruct((lines, width), BF16),
        in_specs=[
            pl.BlockSpec(memory_space=pltpu.HBM),
            pl.BlockSpec(memory_space=pltpu.HBM),
            pl.BlockSpec(memory_space=pltpu.HBM),
        ],
        out_specs=pl.BlockSpec(memory_space=pltpu.VMEM),
        scratch_shapes=[
            pltpu.SMEM((1, count), jnp.int32),
            vmem((chips, lines, width), BF16),
            *[vmem((chips, lines, w), BF16) for w in widths],
            *[vmem((chips - 1, lines, w), BF16) for w in widths],
            *[vmem((lines, w), F32) for w in widths],
            *[vmem((chips - 1, lines, w), BF16) for w in widths],
            *[vmem((lines, w), BF16) for w in widths],
            vmem((slots * whole, lines), BF16),
            vmem((slots, whole, lines), BF16),
            vmem((slots, lines, whole), BF16),
            vmem((slots, 2, width, width), BF16),
            vmem((2, nodes, slots * rows, quarter), BF16),
            vmem((2, nodes, slots * rows, quarter), BF16),
            vmem((slots, nodes, 2 * rows, quarter), BF16),
            vmem((slots, nodes, 2 * rows, quarter), BF16),
            vmem((slots, width, width), BF16),
            vmem((slots, width, width), BF16),
            vmem((width, width), F32),
            vmem((slots, nodes, 2 * rows, cols), BF16),
            vmem((slots, nodes, 2 * rows, cols), BF16),
            vmem((whole, cols), F32),
            dma((3,)), dma((3,)), dma((3,)), dma((3,)),
            dma((2,)), dma((2,)), dma((slots,)), dma((slots,)), dma((slots,)), dma((slots,)),
            dma((3,)), dma, dma, pltpu.SemaphoreType.REGULAR,
        ],
        compiler_params=pltpu.CompilerParams(
            collective_id=0, has_side_effects=True, vmem_limit_bytes=60 << 20
        ),
    )(owners, partials.reshape(chips, 2, lines, width), factors[0, 0])
    return BETA * momentum + update.astype(F32).reshape(momentum.shape)


def solution(mesh):
    placed = (
        P("rep", None, None, "fsdp", None),
        P("rep", None, "fsdp", None),
        P("rep", None),
        P("rep", "fsdp", None, None, None, None),
    )
    return jax.shard_map(
        local, mesh=mesh, in_specs=placed, out_specs=P("rep", None, "fsdp", None), check_vma=False
    )
```

```python
import functools

import jax
import jax.numpy as jnp
from jax import lax
from jax.experimental import pallas as pl
from jax.experimental.pallas import tpu as pltpu
from jax.sharding import PartitionSpec as P

EPSILON = 1e-06
BETA = 0.9
MESH = pl.DeviceIdType.MESH
F32 = jnp.float32
BF16 = jnp.bfloat16


def iota(shape, dim):
    return lax.broadcasted_iota(jnp.int32, shape, dim)


def kernel(
    nodes, count, rows, width, slots,
    own_hbm, part, fac, out,
    owners, mine, sib0, sib1, sib2, psum0, psum1, psum2, own0, own1, own2, xin0, xin1, xin2,
    grad0, grad1, grad2, pick_both, pick_one, pick_in, held, outa, ina, outb, inb,
    block, left, prec, out2, in2, picked,
    sib_send, sib_recv, x_send, x_recv, senda, recva, sendb, recvb, send2, recv2,
    part_sem, fac_sem, own_sem, after_sem, line_sem,
):
    rep = lax.axis_index("rep")
    me = lax.axis_index("fsdp")
    chip, core = rep // 2, lax.rem(rep, 2)
    chips = part.shape[0]
    side = 8
    quarter = width // 4
    cols = width // 2
    lines = count * rows
    whole = nodes * rows
    sibling = {"rep": chip * 2 + 1 - core}
    spans = ((0, quarter), (quarter, quarter), (cols, cols))
    sib, psum, own = (sib0, sib1, sib2), (psum0, psum1, psum2), (own0, own1, own2)
    xin, grad = (xin0, xin1, xin2), (grad0, grad1, grad2)

    def fetch(i):
        span = pl.ds(*spans[i])
        return pltpu.make_async_copy(
            part.at[:, core, :, span], mine.at[:, :, span], part_sem.at[i]
        )

    fetch(0).start()
    ids = pltpu.make_async_copy(own_hbm, owners, own_sem)
    ids.start()

    barrier = pltpu.get_barrier_semaphore()
    pl.semaphore_signal(barrier, inc=1, device_id=sibling, device_id_type=MESH)
    for k in range(1, chips):
        pl.semaphore_signal(
            barrier, inc=1, device_id={"rep": lax.rem(chip + k, chips) * 2 + core},
            device_id_type=MESH,
        )

    y, z = me // side, lax.rem(me, side)

    def peer(at_y, at_z):
        return {"fsdp": at_y * side + at_z}

    half = side // 2
    turn = jnp.where(y < half, y, side + half - 1 - y)

    def at_turn(j):
        return jnp.where(j < half, j, side + half - 1 - j)

    def tell(semaphore, first, last, along_y):
        def one(j, carry):
            to = peer(at_turn(j), z) if along_y else peer(y, j)
            pl.semaphore_signal(semaphore, inc=1, device_id=to, device_id_type=MESH)
            return carry

        lax.fori_loop(first, last, one, 0)

    tell(barrier, z + 1, side, False)
    tell(barrier, turn + 1, side, True)
    pl.semaphore_wait(barrier, 1 + chips - 1 + turn + z)

    def to_sibling(i):
        return pltpu.make_async_remote_copy(
            src_ref=part.at[:, 1 - core, :, pl.ds(*spans[i])],
            dst_ref=sib[i],
            send_sem=sib_send.at[i],
            recv_sem=sib_recv.at[i],
            device_id=sibling,
            device_id_type=MESH,
        )

    for i in range(3):
        to_sibling(i).start()
    for i in range(1, 3):
        fetch(i).start()
    tell(after_sem, 0, z, False)
    tell(after_sem, 0, turn, True)
    load = pltpu.make_async_copy(fac, held, fac_sem)

    def to_chip(i, k):
        return pltpu.make_async_remote_copy(
            src_ref=psum[i].at[k - 1],
            dst_ref=xin[i].at[k - 1],
            send_sem=x_send.at[i],
            recv_sem=x_recv.at[i],
            device_id={"rep": lax.rem(chip + k, chips) * 2 + core},
            device_id_type=MESH,
        )

    def x_bulk(i):
        return pltpu.make_async_remote_copy(
            src_ref=psum[i], dst_ref=xin[i], send_sem=x_send.at[i], recv_sem=x_recv.at[i],
            device_id=sibling, device_id_type=MESH,
        )

    def pair_sums(i):
        span = pl.ds(*spans[i])
        to_sibling(i).wait_recv()
        fetch(i).wait()
        for k in (2, 1, 3):
            other = lax.rem(chip + k, chips)
            pair = mine[other, :, span].astype(F32) + sib[i][other].astype(F32)
            psum[i][k - 1] = pair.astype(BF16)
            if i == 0:
                to_chip(i, k).start()
        own[i][...] = mine[chip, :, span].astype(F32) + sib[i][chip].astype(F32)

    def total(i):
        x_bulk(i).wait_recv()
        if i + 1 < 3:
            for k in (2, 1, 3):
                to_chip(i + 1, k).start()
        acc = own[i][...]
        for k in range(chips - 1):
            acc = acc + xin[i][k].astype(F32)
        grad[i][...] = acc.astype(BF16)

    def send_loop(source, target, send, recv):
        def one(k, carry):
            p = lax.rem(me + k * 27, nodes)
            pltpu.make_async_remote_copy(
                src_ref=source.at[p],
                dst_ref=target.at[me],
                send_sem=send,
                recv_sem=recv,
                device_id={"fsdp": p},
                device_id_type=MESH,
            ).start()
            return carry

        lax.fori_loop(1, nodes, one, 0)

    def bulk(source, target, send, recv):
        most = pl.ds(0, nodes - 1)
        return pltpu.make_async_remote_copy(
            src_ref=source.at[most],
            dst_ref=target.at[most],
            send_sem=send,
            recv_sem=recv,
            device_id={"fsdp": lax.rem(me + 1, nodes)},
            device_id_type=MESH,
        )

    ids.wait()
    lane_block = iota((32, lines), 1) // rows
    sub = iota((32, lines), 0)

    def spread(b, carry):
        lanes, subs = carry
        o = owners[0, b]
        return jnp.where(lane_block == b, o, lanes), jnp.where(sub == b, o, subs)

    own_lane, own_sub = lax.fori_loop(
        0, count, spread, (jnp.zeros((32, lines), jnp.int32), jnp.full((32, lines), -1, jnp.int32))
    )
    earlier = (own_lane == own_sub) & (sub < lane_block)
    slot_lane = jnp.sum(earlier.astype(jnp.int32), axis=0, keepdims=True)
    row_lane = lax.rem(iota((1, lines), 1), rows)
    place = (own_lane[0:1] * slots + slot_lane) * rows + row_lane
    step = 2 * rows * 4

    pair_sums(0)
    load.start()

    def build(i, carry):
        first = pl.multiple_of(i * step, step)
        match = iota((step, lines), 0) + first == place
        pick_both[pl.ds(first, step), :] = jnp.where(match, 1.0, 0.0).astype(BF16)
        return carry

    lax.fori_loop(0, slots * whole // step, build, 0)
    pair_sums(1)

    later = 2 * (side - 1) - turn - z

    @pl.when(later > 0)
    def _():
        pl.semaphore_wait(after_sem, later)

    tell(line_sem, 0, turn, True)
    tell(line_sem, turn + 1, side, True)
    pl.semaphore_wait(line_sem, side - 1)

    for i in range(2):
        total(i)
        outa[i] = jnp.dot(pick_both[...], grad[i][...], preferred_element_type=F32).reshape(
            nodes, slots * rows, quarter
        ).astype(BF16)
        ina[i, me] = outa[i, me]
        send_loop(outa.at[i], ina.at[i], senda.at[i], recva.at[i])
        if i == 0:
            pair_sums(2)

    place_one = own_lane[0:1] * rows + row_lane
    for s in range(slots):
        here = jnp.where(slot_lane == s, place_one, -1)

        def build_one(i, carry, s=s, here=here):
            first = pl.multiple_of(i * step, step)
            match = iota((step, lines), 0) + first == here
            pick_one[s, pl.ds(first, step), :] = jnp.where(match, 1.0, 0.0).astype(BF16)
            return carry

        lax.fori_loop(0, whole // step, build_one, 0)

    total(2)
    for s in range(slots):
        picked[...] = jnp.dot(pick_one[s], grad[2][...], preferred_element_type=F32)
        one = picked[:, :quarter].reshape(nodes, rows, quarter)
        two = picked[:, quarter:].reshape(nodes, rows, quarter)
        outb[s] = jnp.concatenate([one, two], axis=1).astype(BF16)
        inb[s, me] = outb[s, me]
        send_loop(outb.at[s], inb.at[s], sendb.at[s], recvb.at[s])

    row_block = iota((lines, 128), 0) // rows
    lane = iota((lines, 128), 1)

    def spread_rows(b, carry):
        mine_rows, others = carry
        o = owners[0, b]
        return jnp.where(row_block == b, o, mine_rows), jnp.where(lane == b, o, others)

    own_row, own_other = lax.fori_loop(
        0, count, spread_rows,
        (jnp.zeros((lines, 128), jnp.int32), jnp.full((lines, 128), -1, jnp.int32)),
    )
    earlier = (own_row == own_other) & (lane < row_block)
    slot_row = jnp.sum(earlier.astype(jnp.int32), axis=1, keepdims=True)
    place_row = own_row[:, 0:1] * rows + lax.rem(iota((lines, 1), 0), rows)
    for s in range(slots):
        here = jnp.where(slot_row == s, place_row, -1)
        match = iota((lines, whole), 1) == here
        pick_in[s] = jnp.where(match, 1.0, 0.0).astype(BF16)
    load.wait()

    squares = [jnp.zeros((rows, quarter), F32) for _ in range(slots)]
    for i in range(2):
        bulk(outa.at[i], ina.at[i], senda.at[i], recva.at[i]).wait_recv()
        for s in range(slots):
            wide = ina[i][:, s * rows : (s + 1) * rows].astype(F32)
            squares[s] = squares[s] + jnp.sum(wide * wide, axis=0)
            block[s, :, i * quarter : (i + 1) * quarter] = wide.reshape(whole, quarter).astype(BF16)
    for s in range(slots):
        left[s, :, :cols] = jnp.dot(
            held[s, 0], block[s, :, :cols], preferred_element_type=F32
        ).astype(BF16)
    for s in range(slots):
        bulk(outb.at[s], inb.at[s], sendb.at[s], recvb.at[s]).wait_recv()
        for q in range(2):
            wide = inb[s][:, q * rows : (q + 1) * rows].astype(F32)
            squares[s] = squares[s] + jnp.sum(wide * wide, axis=0)
            block[s, :, cols + q * quarter : cols + (q + 1) * quarter] = wide.reshape(
                whole, quarter
            ).astype(BF16)
        left[s, :, cols:] = jnp.dot(
            held[s, 0], block[s, :, cols:], preferred_element_type=F32
        ).astype(BF16)
        prec[...] = jnp.dot(left[s], held[s, 1], preferred_element_type=F32)
        prec_sq = jnp.sum(prec[...] * prec[...], keepdims=True).reshape(1, 1)
        grad_sq = jnp.sum(squares[s], keepdims=True).reshape(1, 1)
        ratio = jnp.sqrt(grad_sq / (prec_sq + EPSILON))
        update = prec[...] * ratio
        one = update[:, :cols].reshape(nodes, rows, cols)
        two = update[:, cols:].reshape(nodes, rows, cols)
        out2[s] = jnp.concatenate([one, two], axis=1).astype(BF16)
        in2[s, me] = out2[s, me]
        send_loop(out2.at[s], in2.at[s], send2.at[s], recv2.at[s])

    for s in range(slots):
        bulk(out2.at[s], in2.at[s], send2.at[s], recv2.at[s]).wait_recv()
        for h in range(2):
            rows_h = in2[s][:, h * rows : (h + 1) * rows].astype(F32).reshape(whole, cols)
            got = jnp.dot(pick_in[s], rows_h.astype(BF16), preferred_element_type=F32)
            if s == 0:
                prec[h * lines : (h + 1) * lines, :cols] = got
            else:
                got = got + prec[h * lines : (h + 1) * lines, :cols]
                out[:, h * cols : (h + 1) * cols] = got.astype(BF16)

    for i in range(3):
        to_sibling(i).wait_send()
        x_bulk(i).wait_send()
    for s in range(2):
        bulk(outa.at[s], ina.at[s], senda.at[s], recva.at[s]).wait_send()
        bulk(outb.at[s], inb.at[s], sendb.at[s], recvb.at[s]).wait_send()
        bulk(out2.at[s], in2.at[s], send2.at[s], recv2.at[s]).wait_send()


def local(partials, momentum, owners, factors):
    nodes = lax.axis_size("fsdp")
    slots = factors.shape[2]
    groups, count, rows, width = partials.shape[1:]
    lines = count * rows
    chips = groups // 2
    cols, quarter = width // 2, width // 4
    whole = nodes * rows
    widths = (quarter, quarter, cols)
    vmem, dma = pltpu.VMEM, pltpu.SemaphoreType.DMA
    update = pl.pallas_call(
        functools.partial(kernel, nodes, count, rows, width, slots),
        out_shape=jax.ShapeDtypeStruct((lines, width), BF16),
        in_specs=[
            pl.BlockSpec(memory_space=pltpu.HBM),
            pl.BlockSpec(memory_space=pltpu.HBM),
            pl.BlockSpec(memory_space=pltpu.HBM),
        ],
        out_specs=pl.BlockSpec(memory_space=pltpu.VMEM),
        scratch_shapes=[
            pltpu.SMEM((1, count), jnp.int32),
            vmem((chips, lines, width), BF16),
            *[vmem((chips, lines, w), BF16) for w in widths],
            *[vmem((chips - 1, lines, w), BF16) for w in widths],
            *[vmem((lines, w), F32) for w in widths],
            *[vmem((chips - 1, lines, w), BF16) for w in widths],
            *[vmem((lines, w), BF16) for w in widths],
            vmem((slots * whole, lines), BF16),
            vmem((slots, whole, lines), BF16),
            vmem((slots, lines, whole), BF16),
            vmem((slots, 2, width, width), BF16),
            vmem((2, nodes, slots * rows, quarter), BF16),
            vmem((2, nodes, slots * rows, quarter), BF16),
            vmem((slots, nodes, 2 * rows, quarter), BF16),
            vmem((slots, nodes, 2 * rows, quarter), BF16),
            vmem((slots, width, width), BF16),
            vmem((slots, width, width), BF16),
            vmem((width, width), F32),
            vmem((slots, nodes, 2 * rows, cols), BF16),
            vmem((slots, nodes, 2 * rows, cols), BF16),
            vmem((whole, cols), F32),
            dma((3,)), dma((3,)), dma((3,)), dma((3,)),
            dma((2,)), dma((2,)), dma((slots,)), dma((slots,)), dma((slots,)), dma((slots,)),
            dma((3,)), dma, dma,
            pltpu.SemaphoreType.REGULAR, pltpu.SemaphoreType.REGULAR,
        ],
        compiler_params=pltpu.CompilerParams(
            collective_id=0, has_side_effects=True, vmem_limit_bytes=53 << 20
        ),
    )(owners, partials.reshape(chips, 2, lines, width), factors[0, 0])
    return BETA * momentum + update.astype(F32).reshape(momentum.shape)


def solution(mesh):
    placed = (
        P("rep", None, None, "fsdp", None),
        P("rep", None, "fsdp", None),
        P("rep", None),
        P("rep", "fsdp", None, None, None, None),
    )
    return jax.shard_map(
        local, mesh=mesh, in_specs=placed, out_specs=P("rep", None, "fsdp", None), check_vma=False
    )
```

```python
import functools

import jax
import jax.numpy as jnp
from jax import lax
from jax.experimental import pallas as pl
from jax.experimental.pallas import tpu as pltpu
from jax.sharding import PartitionSpec as P

EPSILON = 1e-06
BETA = 0.9
MESH = pl.DeviceIdType.MESH
F32 = jnp.float32
BF16 = jnp.bfloat16


def iota(shape, dim):
    return lax.broadcasted_iota(jnp.int32, shape, dim)


def kernel(
    nodes, count, rows, width, slots,
    own_hbm, part, fac, out,
    owners, mine, sib0, sib1, sib2, psum0, psum1, psum2, own0, own1, own2, xin0, xin1, xin2,
    grad0, grad1, grad2, pick_both, pick_one, pick_in, held, outa, ina, outb, inb,
    block, left, prec, out2, in2, picked,
    sib_send, sib_recv, x_send, x_recv, senda, recva, sendb, recvb, send2, recv2,
    part_sem, fac_sem, own_sem, after_sem, line_sem,
):
    rep = lax.axis_index("rep")
    me = lax.axis_index("fsdp")
    chip, core = rep // 2, lax.rem(rep, 2)
    chips = part.shape[0]
    side = 8
    quarter = width // 4
    cols = width // 2
    lines = count * rows
    whole = nodes * rows
    sibling = {"rep": chip * 2 + 1 - core}
    spans = ((0, quarter), (quarter, quarter), (cols, cols))
    sib, psum, own = (sib0, sib1, sib2), (psum0, psum1, psum2), (own0, own1, own2)
    xin, grad = (xin0, xin1, xin2), (grad0, grad1, grad2)

    def fetch(i):
        span = pl.ds(*spans[i])
        return pltpu.make_async_copy(
            part.at[:, core, :, span], mine.at[:, :, span], part_sem.at[i]
        )

    fetch(0).start()
    ids = pltpu.make_async_copy(own_hbm, owners, own_sem)
    ids.start()

    barrier = pltpu.get_barrier_semaphore()
    pl.semaphore_signal(barrier, inc=1, device_id=sibling, device_id_type=MESH)
    for k in range(1, chips):
        pl.semaphore_signal(
            barrier, inc=1, device_id={"rep": lax.rem(chip + k, chips) * 2 + core},
            device_id_type=MESH,
        )

    y, z = me // side, lax.rem(me, side)

    def peer(at_y, at_z):
        return {"fsdp": at_y * side + at_z}

    half = side // 2
    turn = jnp.where(y < half, y, side + half - 1 - y)

    def at_turn(j):
        return jnp.where(j < half, j, side + half - 1 - j)

    def tell(semaphore, first, last, along_y):
        def one(j, carry):
            to = peer(at_turn(j), z) if along_y else peer(y, j)
            pl.semaphore_signal(semaphore, inc=1, device_id=to, device_id_type=MESH)
            return carry

        lax.fori_loop(first, last, one, 0)

    tell(barrier, z + 1, side, False)
    tell(barrier, turn + 1, side, True)
    pl.semaphore_wait(barrier, 1 + chips - 1 + turn + z)

    def to_sibling(i):
        return pltpu.make_async_remote_copy(
            src_ref=part.at[:, 1 - core, :, pl.ds(*spans[i])],
            dst_ref=sib[i],
            send_sem=sib_send.at[i],
            recv_sem=sib_recv.at[i],
            device_id=sibling,
            device_id_type=MESH,
        )

    for i in range(3):
        to_sibling(i).start()
    for i in range(1, 3):
        fetch(i).start()
    tell(after_sem, 0, z, False)
    tell(after_sem, 0, turn, True)
    load = pltpu.make_async_copy(fac, held, fac_sem)

    def to_chip(i, k):
        return pltpu.make_async_remote_copy(
            src_ref=psum[i].at[k - 1],
            dst_ref=xin[i].at[k - 1],
            send_sem=x_send.at[i],
            recv_sem=x_recv.at[i],
            device_id={"rep": lax.rem(chip + k, chips) * 2 + core},
            device_id_type=MESH,
        )

    def x_bulk(i):
        return pltpu.make_async_remote_copy(
            src_ref=psum[i], dst_ref=xin[i], send_sem=x_send.at[i], recv_sem=x_recv.at[i],
            device_id=sibling, device_id_type=MESH,
        )

    def pair_sums(i):
        span = pl.ds(*spans[i])
        to_sibling(i).wait_recv()
        fetch(i).wait()
        for k in (2, 1, 3):
            other = lax.rem(chip + k, chips)
            pair = mine[other, :, span].astype(F32) + sib[i][other].astype(F32)
            psum[i][k - 1] = pair.astype(BF16)
            if i == 0:
                to_chip(i, k).start()
        own[i][...] = mine[chip, :, span].astype(F32) + sib[i][chip].astype(F32)

    def total(i):
        x_bulk(i).wait_recv()
        if i + 1 < 3:
            for k in (2, 1, 3):
                to_chip(i + 1, k).start()
        acc = own[i][...]
        for k in range(chips - 1):
            acc = acc + xin[i][k].astype(F32)
        grad[i][...] = acc.astype(BF16)

    def send_loop(source, target, send, recv):
        def one(k, carry):
            o = lax.rem(k * 27, nodes)
            p = lax.rem(y + o // side, side) * side + lax.rem(z + o, side)
            pltpu.make_async_remote_copy(
                src_ref=source.at[p],
                dst_ref=target.at[me],
                send_sem=send,
                recv_sem=recv,
                device_id={"fsdp": p},
                device_id_type=MESH,
            ).start()
            return carry

        lax.fori_loop(1, nodes, one, 0)

    def bulk(source, target, send, recv):
        most = pl.ds(0, nodes - 1)
        return pltpu.make_async_remote_copy(
            src_ref=source.at[most],
            dst_ref=target.at[most],
            send_sem=send,
            recv_sem=recv,
            device_id={"fsdp": lax.rem(me + 1, nodes)},
            device_id_type=MESH,
        )

    ids.wait()
    lane_block = iota((32, lines), 1) // rows
    sub = iota((32, lines), 0)

    def spread(b, carry):
        lanes, subs = carry
        o = owners[0, b]
        return jnp.where(lane_block == b, o, lanes), jnp.where(sub == b, o, subs)

    own_lane, own_sub = lax.fori_loop(
        0, count, spread, (jnp.zeros((32, lines), jnp.int32), jnp.full((32, lines), -1, jnp.int32))
    )
    earlier = (own_lane == own_sub) & (sub < lane_block)
    slot_lane = jnp.sum(earlier.astype(jnp.int32), axis=0, keepdims=True)
    row_lane = lax.rem(iota((1, lines), 1), rows)
    place = (own_lane[0:1] * slots + slot_lane) * rows + row_lane
    step = 2 * rows * 4

    pair_sums(0)
    load.start()

    def build(i, carry):
        first = pl.multiple_of(i * step, step)
        match = iota((step, lines), 0) + first == place
        pick_both[pl.ds(first, step), :] = jnp.where(match, 1.0, 0.0).astype(BF16)
        return carry

    lax.fori_loop(0, slots * whole // step, build, 0)
    pair_sums(1)

    later = 2 * (side - 1) - turn - z

    @pl.when(later > 0)
    def _():
        pl.semaphore_wait(after_sem, later)

    tell(line_sem, 0, turn, True)
    tell(line_sem, turn + 1, side, True)
    pl.semaphore_wait(line_sem, side - 1)

    for i in range(2):
        total(i)
        outa[i] = jnp.dot(pick_both[...], grad[i][...], preferred_element_type=F32).reshape(
            nodes, slots * rows, quarter
        ).astype(BF16)
        ina[i, me] = outa[i, me]
        send_loop(outa.at[i], ina.at[i], senda.at[i], recva.at[i])
        if i == 0:
            pair_sums(2)

    place_one = own_lane[0:1] * rows + row_lane
    for s in range(slots):
        here = jnp.where(slot_lane == s, place_one, -1)

        def build_one(i, carry, s=s, here=here):
            first = pl.multiple_of(i * step, step)
            match = iota((step, lines), 0) + first == here
            pick_one[s, pl.ds(first, step), :] = jnp.where(match, 1.0, 0.0).astype(BF16)
            return carry

        lax.fori_loop(0, whole // step, build_one, 0)

    total(2)
    for s in range(slots):
        picked[...] = jnp.dot(pick_one[s], grad[2][...], preferred_element_type=F32)
        one = picked[:, :quarter].reshape(nodes, rows, quarter)
        two = picked[:, quarter:].reshape(nodes, rows, quarter)
        outb[s] = jnp.concatenate([one, two], axis=1).astype(BF16)
        inb[s, me] = outb[s, me]
        send_loop(outb.at[s], inb.at[s], sendb.at[s], recvb.at[s])

    row_block = iota((lines, 128), 0) // rows
    lane = iota((lines, 128), 1)

    def spread_rows(b, carry):
        mine_rows, others = carry
        o = owners[0, b]
        return jnp.where(row_block == b, o, mine_rows), jnp.where(lane == b, o, others)

    own_row, own_other = lax.fori_loop(
        0, count, spread_rows,
        (jnp.zeros((lines, 128), jnp.int32), jnp.full((lines, 128), -1, jnp.int32)),
    )
    earlier = (own_row == own_other) & (lane < row_block)
    slot_row = jnp.sum(earlier.astype(jnp.int32), axis=1, keepdims=True)
    place_row = own_row[:, 0:1] * rows + lax.rem(iota((lines, 1), 0), rows)
    for s in range(slots):
        here = jnp.where(slot_row == s, place_row, -1)
        match = iota((lines, whole), 1) == here
        pick_in[s] = jnp.where(match, 1.0, 0.0).astype(BF16)
    load.wait()

    squares = [jnp.zeros((rows, quarter), F32) for _ in range(slots)]
    for i in range(2):
        bulk(outa.at[i], ina.at[i], senda.at[i], recva.at[i]).wait_recv()
        for s in range(slots):
            wide = ina[i][:, s * rows : (s + 1) * rows].astype(F32)
            squares[s] = squares[s] + jnp.sum(wide * wide, axis=0)
            block[s, :, i * quarter : (i + 1) * quarter] = wide.reshape(whole, quarter).astype(BF16)
    for s in range(slots):
        left[s, :, :cols] = jnp.dot(
            held[s, 0], block[s, :, :cols], preferred_element_type=F32
        ).astype(BF16)
    for s in range(slots):
        bulk(outb.at[s], inb.at[s], sendb.at[s], recvb.at[s]).wait_recv()
        for q in range(2):
            wide = inb[s][:, q * rows : (q + 1) * rows].astype(F32)
            squares[s] = squares[s] + jnp.sum(wide * wide, axis=0)
            block[s, :, cols + q * quarter : cols + (q + 1) * quarter] = wide.reshape(
                whole, quarter
            ).astype(BF16)
        left[s, :, cols:] = jnp.dot(
            held[s, 0], block[s, :, cols:], preferred_element_type=F32
        ).astype(BF16)
        prec[...] = jnp.dot(left[s], held[s, 1], preferred_element_type=F32)
        prec_sq = jnp.sum(prec[...] * prec[...], keepdims=True).reshape(1, 1)
        grad_sq = jnp.sum(squares[s], keepdims=True).reshape(1, 1)
        ratio = jnp.sqrt(grad_sq / (prec_sq + EPSILON))
        update = prec[...] * ratio
        one = update[:, :cols].reshape(nodes, rows, cols)
        two = update[:, cols:].reshape(nodes, rows, cols)
        out2[s] = jnp.concatenate([one, two], axis=1).astype(BF16)
        in2[s, me] = out2[s, me]
        send_loop(out2.at[s], in2.at[s], send2.at[s], recv2.at[s])

    for s in range(slots):
        bulk(out2.at[s], in2.at[s], send2.at[s], recv2.at[s]).wait_recv()
        for h in range(2):
            rows_h = in2[s][:, h * rows : (h + 1) * rows].astype(F32).reshape(whole, cols)
            got = jnp.dot(pick_in[s], rows_h.astype(BF16), preferred_element_type=F32)
            if s == 0:
                prec[h * lines : (h + 1) * lines, :cols] = got
            else:
                got = got + prec[h * lines : (h + 1) * lines, :cols]
                out[:, h * cols : (h + 1) * cols] = got.astype(BF16)

    for i in range(3):
        to_sibling(i).wait_send()
        x_bulk(i).wait_send()
    for s in range(2):
        bulk(outa.at[s], ina.at[s], senda.at[s], recva.at[s]).wait_send()
        bulk(outb.at[s], inb.at[s], sendb.at[s], recvb.at[s]).wait_send()
        bulk(out2.at[s], in2.at[s], send2.at[s], recv2.at[s]).wait_send()


def local(partials, momentum, owners, factors):
    nodes = lax.axis_size("fsdp")
    slots = factors.shape[2]
    groups, count, rows, width = partials.shape[1:]
    lines = count * rows
    chips = groups // 2
    cols, quarter = width // 2, width // 4
    whole = nodes * rows
    widths = (quarter, quarter, cols)
    vmem, dma = pltpu.VMEM, pltpu.SemaphoreType.DMA
    update = pl.pallas_call(
        functools.partial(kernel, nodes, count, rows, width, slots),
        out_shape=jax.ShapeDtypeStruct((lines, width), BF16),
        in_specs=[
            pl.BlockSpec(memory_space=pltpu.HBM),
            pl.BlockSpec(memory_space=pltpu.HBM),
            pl.BlockSpec(memory_space=pltpu.HBM),
        ],
        out_specs=pl.BlockSpec(memory_space=pltpu.VMEM),
        scratch_shapes=[
            pltpu.SMEM((1, count), jnp.int32),
            vmem((chips, lines, width), BF16),
            *[vmem((chips, lines, w), BF16) for w in widths],
            *[vmem((chips - 1, lines, w), BF16) for w in widths],
            *[vmem((lines, w), F32) for w in widths],
            *[vmem((chips - 1, lines, w), BF16) for w in widths],
            *[vmem((lines, w), BF16) for w in widths],
            vmem((slots * whole, lines), BF16),
            vmem((slots, whole, lines), BF16),
            vmem((slots, lines, whole), BF16),
            vmem((slots, 2, width, width), BF16),
            vmem((2, nodes, slots * rows, quarter), BF16),
            vmem((2, nodes, slots * rows, quarter), BF16),
            vmem((slots, nodes, 2 * rows, quarter), BF16),
            vmem((slots, nodes, 2 * rows, quarter), BF16),
            vmem((slots, width, width), BF16),
            vmem((slots, width, width), BF16),
            vmem((width, width), F32),
            vmem((slots, nodes, 2 * rows, cols), BF16),
            vmem((slots, nodes, 2 * rows, cols), BF16),
            vmem((whole, cols), F32),
            dma((3,)), dma((3,)), dma((3,)), dma((3,)),
            dma((2,)), dma((2,)), dma((slots,)), dma((slots,)), dma((slots,)), dma((slots,)),
            dma((3,)), dma, dma,
            pltpu.SemaphoreType.REGULAR, pltpu.SemaphoreType.REGULAR,
        ],
        compiler_params=pltpu.CompilerParams(
            collective_id=0, has_side_effects=True, vmem_limit_bytes=53 << 20
        ),
    )(owners, partials.reshape(chips, 2, lines, width), factors[0, 0])
    return BETA * momentum + update.astype(F32).reshape(momentum.shape)


def solution(mesh):
    placed = (
        P("rep", None, None, "fsdp", None),
        P("rep", None, "fsdp", None),
        P("rep", None),
        P("rep", "fsdp", None, None, None, None),
    )
    return jax.shard_map(
        local, mesh=mesh, in_specs=placed, out_specs=P("rep", None, "fsdp", None), check_vma=False
    )
```

```python
import functools

import jax
import jax.numpy as jnp
from jax import lax
from jax.experimental import pallas as pl
from jax.experimental.pallas import tpu as pltpu
from jax.sharding import PartitionSpec as P

EPSILON = 1e-06
BETA = 0.9
MESH = pl.DeviceIdType.MESH
F32 = jnp.float32
BF16 = jnp.bfloat16


def iota(shape, dim):
    return lax.broadcasted_iota(jnp.int32, shape, dim)


def kernel(
    nodes, count, rows, width, slots,
    own_hbm, part, fac, out,
    owners, mine, sib0, sib1, sib2, psum0, psum1, psum2, own0, own1, own2, xin0, xin1, xin2,
    grad0, grad1, grad2, pick_both, pick_one, pick_in, held, outa, ina, outb, inb,
    block, left, prec, out2, in2, picked,
    sib_send, sib_recv, x_send, x_recv, senda, recva, sendb, recvb, send2, recv2,
    part_sem, fac_sem, own_sem, after_sem, line_sem,
):
    rep = lax.axis_index("rep")
    me = lax.axis_index("fsdp")
    chip, core = rep // 2, lax.rem(rep, 2)
    chips = part.shape[0]
    side = 8
    quarter = width // 4
    cols = width // 2
    lines = count * rows
    whole = nodes * rows
    sibling = {"rep": chip * 2 + 1 - core}
    spans = ((0, quarter), (quarter, quarter), (cols, cols))
    sib, psum, own = (sib0, sib1, sib2), (psum0, psum1, psum2), (own0, own1, own2)
    xin, grad = (xin0, xin1, xin2), (grad0, grad1, grad2)

    def fetch(i):
        span = pl.ds(*spans[i])
        return pltpu.make_async_copy(
            part.at[:, core, :, span], mine.at[:, :, span], part_sem.at[i]
        )

    fetch(0).start()
    ids = pltpu.make_async_copy(own_hbm, owners, own_sem)
    ids.start()

    barrier = pltpu.get_barrier_semaphore()
    pl.semaphore_signal(barrier, inc=1, device_id=sibling, device_id_type=MESH)
    for k in range(1, chips):
        pl.semaphore_signal(
            barrier, inc=1, device_id={"rep": lax.rem(chip + k, chips) * 2 + core},
            device_id_type=MESH,
        )

    y, z = me // side, lax.rem(me, side)

    def peer(at_y, at_z):
        return {"fsdp": at_y * side + at_z}

    half = side // 2
    turn = jnp.where(y < half, y, side + half - 1 - y)

    def at_turn(j):
        return jnp.where(j < half, j, side + half - 1 - j)

    def tell(semaphore, first, last, along_y):
        def one(j, carry):
            to = peer(at_turn(j), z) if along_y else peer(y, j)
            pl.semaphore_signal(semaphore, inc=1, device_id=to, device_id_type=MESH)
            return carry

        lax.fori_loop(first, last, one, 0)

    tell(barrier, z + 1, side, False)
    tell(barrier, turn + 1, side, True)
    pl.semaphore_wait(barrier, 1 + chips - 1 + turn + z)

    def to_sibling(i):
        return pltpu.make_async_remote_copy(
            src_ref=part.at[:, 1 - core, :, pl.ds(*spans[i])],
            dst_ref=sib[i],
            send_sem=sib_send.at[i],
            recv_sem=sib_recv.at[i],
            device_id=sibling,
            device_id_type=MESH,
        )

    for i in range(3):
        to_sibling(i).start()
    for i in range(1, 3):
        fetch(i).start()
    tell(after_sem, 0, z, False)
    tell(after_sem, 0, turn, True)
    load = pltpu.make_async_copy(fac, held, fac_sem)

    def to_chip(i, k):
        return pltpu.make_async_remote_copy(
            src_ref=psum[i].at[k - 1],
            dst_ref=xin[i].at[k - 1],
            send_sem=x_send.at[i],
            recv_sem=x_recv.at[i],
            device_id={"rep": lax.rem(chip + k, chips) * 2 + core},
            device_id_type=MESH,
        )

    def x_bulk(i):
        return pltpu.make_async_remote_copy(
            src_ref=psum[i], dst_ref=xin[i], send_sem=x_send.at[i], recv_sem=x_recv.at[i],
            device_id=sibling, device_id_type=MESH,
        )

    def pair_sums(i):
        span = pl.ds(*spans[i])
        to_sibling(i).wait_recv()
        fetch(i).wait()
        for k in (2, 1, 3):
            other = lax.rem(chip + k, chips)
            pair = mine[other, :, span].astype(F32) + sib[i][other].astype(F32)
            psum[i][k - 1] = pair.astype(BF16)
            if i == 0:
                to_chip(i, k).start()
        own[i][...] = mine[chip, :, span].astype(F32) + sib[i][chip].astype(F32)

    def total(i):
        x_bulk(i).wait_recv()
        if i + 1 < 3:
            for k in (2, 1, 3):
                to_chip(i + 1, k).start()
        acc = own[i][...]
        for k in range(chips - 1):
            acc = acc + xin[i][k].astype(F32)
        grad[i][...] = acc.astype(BF16)

    def send_loop(source, target, send, recv):
        def one(k, carry):
            o = lax.rem(k * 27, nodes)
            p = lax.rem(y + o // side, side) * side + lax.rem(z + o, side)
            pltpu.make_async_remote_copy(
                src_ref=source.at[p],
                dst_ref=target.at[me],
                send_sem=send,
                recv_sem=recv,
                device_id={"fsdp": p},
                device_id_type=MESH,
            ).start()
            return carry

        lax.fori_loop(1, nodes, one, 0)

    def bulk(source, target, send, recv):
        most = pl.ds(0, nodes - 1)
        return pltpu.make_async_remote_copy(
            src_ref=source.at[most],
            dst_ref=target.at[most],
            send_sem=send,
            recv_sem=recv,
            device_id={"fsdp": lax.rem(me + 1, nodes)},
            device_id_type=MESH,
        )

    pair_sums(0)
    load.start()

    ids.wait()
    lane_block = iota((32, lines), 1) // rows
    sub = iota((32, lines), 0)

    def spread(b, carry):
        lanes, subs = carry
        o = owners[0, b]
        return jnp.where(lane_block == b, o, lanes), jnp.where(sub == b, o, subs)

    own_lane, own_sub = lax.fori_loop(
        0, count, spread, (jnp.zeros((32, lines), jnp.int32), jnp.full((32, lines), -1, jnp.int32))
    )
    earlier = (own_lane == own_sub) & (sub < lane_block)
    slot_lane = jnp.sum(earlier.astype(jnp.int32), axis=0, keepdims=True)
    row_lane = lax.rem(iota((1, lines), 1), rows)
    place = (own_lane[0:1] * slots + slot_lane) * rows + row_lane
    step = 2 * rows * 4

    def build(i, carry):
        first = pl.multiple_of(i * step, step)
        match = iota((step, lines), 0) + first == place
        pick_both[pl.ds(first, step), :] = jnp.where(match, 1.0, 0.0).astype(BF16)
        return carry

    lax.fori_loop(0, slots * whole // step, build, 0)
    pair_sums(1)

    later = 2 * (side - 1) - turn - z

    @pl.when(later > 0)
    def _():
        pl.semaphore_wait(after_sem, later)

    tell(line_sem, 0, turn, True)
    tell(line_sem, turn + 1, side, True)
    pl.semaphore_wait(line_sem, side - 1)

    for i in range(2):
        total(i)
        outa[i] = jnp.dot(pick_both[...], grad[i][...], preferred_element_type=F32).reshape(
            nodes, slots * rows, quarter
        ).astype(BF16)
        ina[i, me] = outa[i, me]
        send_loop(outa.at[i], ina.at[i], senda.at[i], recva.at[i])
        if i == 0:
            pair_sums(2)

    place_one = own_lane[0:1] * rows + row_lane
    for s in range(slots):
        here = jnp.where(slot_lane == s, place_one, -1)

        def build_one(i, carry, s=s, here=here):
            first = pl.multiple_of(i * step, step)
            match = iota((step, lines), 0) + first == here
            pick_one[s, pl.ds(first, step), :] = jnp.where(match, 1.0, 0.0).astype(BF16)
            return carry

        lax.fori_loop(0, whole // step, build_one, 0)

    total(2)
    for s in range(slots):
        picked[...] = jnp.dot(pick_one[s], grad[2][...], preferred_element_type=F32)
        one = picked[:, :quarter].reshape(nodes, rows, quarter)
        two = picked[:, quarter:].reshape(nodes, rows, quarter)
        outb[s] = jnp.concatenate([one, two], axis=1).astype(BF16)
        inb[s, me] = outb[s, me]
        send_loop(outb.at[s], inb.at[s], sendb.at[s], recvb.at[s])

    row_block = iota((lines, 128), 0) // rows
    lane = iota((lines, 128), 1)

    def spread_rows(b, carry):
        mine_rows, others = carry
        o = owners[0, b]
        return jnp.where(row_block == b, o, mine_rows), jnp.where(lane == b, o, others)

    own_row, own_other = lax.fori_loop(
        0, count, spread_rows,
        (jnp.zeros((lines, 128), jnp.int32), jnp.full((lines, 128), -1, jnp.int32)),
    )
    earlier = (own_row == own_other) & (lane < row_block)
    slot_row = jnp.sum(earlier.astype(jnp.int32), axis=1, keepdims=True)
    place_row = own_row[:, 0:1] * rows + lax.rem(iota((lines, 1), 0), rows)
    for s in range(slots):
        here = jnp.where(slot_row == s, place_row, -1)
        match = iota((lines, whole), 1) == here
        pick_in[s] = jnp.where(match, 1.0, 0.0).astype(BF16)
    load.wait()

    squares = [jnp.zeros((rows, quarter), F32) for _ in range(slots)]
    for i in range(2):
        bulk(outa.at[i], ina.at[i], senda.at[i], recva.at[i]).wait_recv()
        for s in range(slots):
            wide = ina[i][:, s * rows : (s + 1) * rows].astype(F32)
            squares[s] = squares[s] + jnp.sum(wide * wide, axis=0)
            block[s, :, i * quarter : (i + 1) * quarter] = wide.reshape(whole, quarter).astype(BF16)
    for s in range(slots):
        left[s, :, :cols] = jnp.dot(
            held[s, 0], block[s, :, :cols], preferred_element_type=F32
        ).astype(BF16)
    for s in range(slots):
        bulk(outb.at[s], inb.at[s], sendb.at[s], recvb.at[s]).wait_recv()
        for q in range(2):
            wide = inb[s][:, q * rows : (q + 1) * rows].astype(F32)
            squares[s] = squares[s] + jnp.sum(wide * wide, axis=0)
            block[s, :, cols + q * quarter : cols + (q + 1) * quarter] = wide.reshape(
                whole, quarter
            ).astype(BF16)
        left[s, :, cols:] = jnp.dot(
            held[s, 0], block[s, :, cols:], preferred_element_type=F32
        ).astype(BF16)
        prec[...] = jnp.dot(left[s], held[s, 1], preferred_element_type=F32)
        prec_sq = jnp.sum(prec[...] * prec[...], keepdims=True).reshape(1, 1)
        grad_sq = jnp.sum(squares[s], keepdims=True).reshape(1, 1)
        ratio = jnp.sqrt(grad_sq / (prec_sq + EPSILON))
        update = prec[...] * ratio
        one = update[:, :cols].reshape(nodes, rows, cols)
        two = update[:, cols:].reshape(nodes, rows, cols)
        out2[s] = jnp.concatenate([one, two], axis=1).astype(BF16)
        in2[s, me] = out2[s, me]
        send_loop(out2.at[s], in2.at[s], send2.at[s], recv2.at[s])

    for s in range(slots):
        bulk(out2.at[s], in2.at[s], send2.at[s], recv2.at[s]).wait_recv()
        for h in range(2):
            rows_h = in2[s][:, h * rows : (h + 1) * rows].astype(F32).reshape(whole, cols)
            got = jnp.dot(pick_in[s], rows_h.astype(BF16), preferred_element_type=F32)
            if s == 0:
                prec[h * lines : (h + 1) * lines, :cols] = got
            else:
                got = got + prec[h * lines : (h + 1) * lines, :cols]
                out[:, h * cols : (h + 1) * cols] = got.astype(BF16)

    for i in range(3):
        to_sibling(i).wait_send()
        x_bulk(i).wait_send()
    for s in range(2):
        bulk(outa.at[s], ina.at[s], senda.at[s], recva.at[s]).wait_send()
        bulk(outb.at[s], inb.at[s], sendb.at[s], recvb.at[s]).wait_send()
        bulk(out2.at[s], in2.at[s], send2.at[s], recv2.at[s]).wait_send()


def local(partials, momentum, owners, factors):
    nodes = lax.axis_size("fsdp")
    slots = factors.shape[2]
    groups, count, rows, width = partials.shape[1:]
    lines = count * rows
    chips = groups // 2
    cols, quarter = width // 2, width // 4
    whole = nodes * rows
    widths = (quarter, quarter, cols)
    vmem, dma = pltpu.VMEM, pltpu.SemaphoreType.DMA
    update = pl.pallas_call(
        functools.partial(kernel, nodes, count, rows, width, slots),
        out_shape=jax.ShapeDtypeStruct((lines, width), BF16),
        in_specs=[
            pl.BlockSpec(memory_space=pltpu.HBM),
            pl.BlockSpec(memory_space=pltpu.HBM),
            pl.BlockSpec(memory_space=pltpu.HBM),
        ],
        out_specs=pl.BlockSpec(memory_space=pltpu.VMEM),
        scratch_shapes=[
            pltpu.SMEM((1, count), jnp.int32),
            vmem((chips, lines, width), BF16),
            *[vmem((chips, lines, w), BF16) for w in widths],
            *[vmem((chips - 1, lines, w), BF16) for w in widths],
            *[vmem((lines, w), F32) for w in widths],
            *[vmem((chips - 1, lines, w), BF16) for w in widths],
            *[vmem((lines, w), BF16) for w in widths],
            vmem((slots * whole, lines), BF16),
            vmem((slots, whole, lines), BF16),
            vmem((slots, lines, whole), BF16),
            vmem((slots, 2, width, width), BF16),
            vmem((2, nodes, slots * rows, quarter), BF16),
            vmem((2, nodes, slots * rows, quarter), BF16),
            vmem((slots, nodes, 2 * rows, quarter), BF16),
            vmem((slots, nodes, 2 * rows, quarter), BF16),
            vmem((slots, width, width), BF16),
            vmem((slots, width, width), BF16),
            vmem((width, width), F32),
            vmem((slots, nodes, 2 * rows, cols), BF16),
            vmem((slots, nodes, 2 * rows, cols), BF16),
            vmem((whole, cols), F32),
            dma((3,)), dma((3,)), dma((3,)), dma((3,)),
            dma((2,)), dma((2,)), dma((slots,)), dma((slots,)), dma((slots,)), dma((slots,)),
            dma((3,)), dma, dma,
            pltpu.SemaphoreType.REGULAR, pltpu.SemaphoreType.REGULAR,
        ],
        compiler_params=pltpu.CompilerParams(
            collective_id=0, has_side_effects=True, vmem_limit_bytes=53 << 20
        ),
    )(owners, partials.reshape(chips, 2, lines, width), factors[0, 0])
    return BETA * momentum + update.astype(F32).reshape(momentum.shape)


def solution(mesh):
    placed = (
        P("rep", None, None, "fsdp", None),
        P("rep", None, "fsdp", None),
        P("rep", None),
        P("rep", "fsdp", None, None, None, None),
    )
    return jax.shard_map(
        local, mesh=mesh, in_specs=placed, out_specs=P("rep", None, "fsdp", None), check_vma=False
    )
```
